32 devices in a mesh: tm: 2 (over core), uv: 16 (over z, y, x).
Axes of the slice: x: 2, y: 2, z: 4, core: 2. Of those that a mesh axis runs over, the one named last changes fastest.
Arguments:
- visibilities: bfloat16 [8, 16, 2, 2, 32768], P(None, 'tm', None, None, 'uv'), may hold values from -6 to 6
- u_offset: float32 [2, 8, 32768], P('tm', None, 'uv'), may hold values from 0 to 128
- v_offset: float32 [2, 8, 32768], P('tm', None, 'uv'), may hold values from 0 to 512
- block_owner: int32 [2, 2048, 1], P('tm', 'uv'), may hold values from 0 to 15; in each aligned block of 128 rows (0 to 127, 128 to 255, ..., all dimensions but the last counted through in order) at most 24 rows name the same one
- block_u_tile: int32 [2, 2048], P('tm', 'uv'), may hold values from 0 to 63
- block_count: int32 [2, 2048], P('tm', 'uv'), may hold values from 16 to 128
- sk_window: int32 [2, 2], P('tm'), may hold values from 300 to 2200, as said below
Outputs:
- dirty_image: float32 [2, 4096, 4096], P('tm', 'uv')
The draws below stay inside these ranges and needn't reach their ends.
Inputs may be any that keep to these rules, and one draw needn't show every extreme that they name: `block_owner`: in each channel, the blocks of one index of uv name no band more than 24 times, a bound that some block reaches. `sk_window`: the lower limit lies from 300 to 600 and the upper from 1600 to 2200; in every draw some channel's lower limit is exactly 300 and some channel's upper limit exactly 2200.
All inputs are finite; a program needn't handle non-finite values.
Results may differ from the reference program's by a relative error of at most 0.0053.
Values sent between devices are 32-bit elements; how exact they have to be, the bound alone decides.
A program may use at most 128 MiB of HBM per device.

```python
import math
import jax
import jax.numpy as jnp
import numpy as np
from jax import lax

NG = 8192
TILE = 128
VISIBILITY_ROWS = 128
CH = 2
SUBS = 16
NBIN = 8
BL_DEV = 2048
NI = 4096
BAND = 512
TILES = 64
BL = 32768
BLK_DEV = 128
BLOCKS = 2048
MOST = 24
N_UV = 16


def draw_sk_window(key, part):
    lower_key, upper_key, pick_key = jax.random.split(jax.random.fold_in(key, 11), 3)
    lower = jax.random.randint(lower_key, (CH,), 300, 601)
    upper = jax.random.randint(upper_key, (CH,), 1600, 2201)
    picks = jax.random.randint(pick_key, (2,), 0, CH)
    channel_ids = jnp.arange(CH)
    lower = jnp.where(channel_ids == picks[0], 300, lower)
    upper = jnp.where(channel_ids == picks[1], 2200, upper)
    return jnp.stack([lower, upper], axis=1).astype(jnp.int32)


def with_ends(result, key, smallest, high):
    longest = result.shape.index(max(result.shape))
    spots = []
    for shift in (0, 1):
        where = [jax.random.randint(jax.random.fold_in(key, axis), (), 0, length) for axis, length in enumerate(result.shape)]
        where[longest] = (where[longest] + shift) % result.shape[longest]
        spots.append(tuple(where))
    return result.at[spots[0]].set(smallest).at[spots[1]].set(high)


def block_scale(rng, extent, shards, least, top_value):
    def one(axis_at, shards_of):
        steps = jax.random.uniform(jax.random.fold_in(jax.random.fold_in(rng, 6), axis_at), (shards_of,), jnp.float32, least / len(shards), top_value / len(shards))
        return jnp.repeat(jnp.exp(steps), extent[axis_at] // shards_of).reshape((-1,) + (1,) * (len(extent) - axis_at - 1))

    gain = one(*shards[0])
    for cut in shards[1:]:
        gain = gain * one(*cut)
    return gain


def shared_out(stream_key, own, number, rows, number_of, top, reach, lean):
    order = jax.random.permutation(stream_key, number_of)
    packed, usual = shares(number_of, rows * top, reach, lean, True), shares(number_of, rows * top, reach, lean, False)
    places = jnp.arange(number_of)

    def named(lengths, turn):
        used = int((lengths > 0).sum())
        fixed = max(1, used // 4)
        moved = fixed + (places - fixed + turn * (used - fixed)) % max(1, number_of - fixed)
        return jnp.zeros((number_of,), jnp.int32).at[order[jnp.where(places < fixed, places, moved)]].set(jnp.asarray(lengths, jnp.int32))

    lengths = jnp.where(number % 4 == 0, named(packed, number // 4), named(usual, number - number // 4 - 1))
    mixed = jax.random.permutation(jax.random.fold_in(own, 3), number_of)
    donor, sink = mixed[0:number_of // 2 * 2:2], mixed[1:number_of // 2 * 2:2]
    margin = jnp.minimum(lengths[donor] - 1, reach - lengths[sink]) // 2
    margin = jnp.where((donor == order[0]) | (sink == order[0]) | (lengths[sink] == 0), 0, jnp.maximum(margin, 0))
    moved = jax.random.randint(jax.random.fold_in(own, 4), (number_of // 2,), 0, 1 << 20) % (margin + 1)
    lengths = lengths.at[donor].add(-moved).at[sink].add(moved)
    items = jnp.searchsorted(jnp.cumsum(lengths), jnp.arange(rows * top), side="right").astype(jnp.int32)
    table = items.reshape(top, rows).T
    table = table[jax.random.permutation(jax.random.fold_in(own, 1), rows)]
    turn = jax.random.randint(jax.random.fold_in(own, 2), (rows, 1), 0, top)
    return jnp.take_along_axis(table, (jnp.arange(top)[None, :] + turn) % top, axis=1)


def shares(number_of, total, most, slope, full):
    weights = [(1 << 20) // math.isqrt(rank ** slope) + 1 for rank in range(1, number_of + 1)]
    largest = most if full else min(most, max(-(-total // number_of), total * weights[0] // sum(weights)))
    least = 1 if total - largest >= number_of - 1 else 0
    counts, surplus = [largest] + [least] * (number_of - 1), total - largest - least * (number_of - 1)
    while surplus > 0:
        free = [i for i in range(1, number_of) if counts[i] < largest] or [i for i in range(1, number_of) if counts[i] < most]
        whole, remaining = sum([weights[i] for i in free]), surplus
        for i in free:
            more = min(most - counts[i], max(1, remaining * weights[i] // whole), surplus)
            counts[i] = counts[i] + more
            surplus = surplus - more
    return np.array(counts)


def centred(own_key, extent, width, reach, cuts=(), kind=jnp.bfloat16):
    factor_of = block_scale(own_key, extent, cuts, -0.22, 0.18) if cuts else 1.0
    entries = jax.random.normal(own_key, extent, jnp.float32) * width * factor_of
    return jnp.minimum(jnp.maximum(entries, -reach), reach).astype(kind)


def setup_inputs(seed: int = 0) -> dict:
    key_of = jax.random.split(jax.random.key(seed), 8)
    visibilities = centred(key_of[0], (NBIN, SUBS, CH, 2, BL), 1.0, 6.0, ((1, 2), (4, 16)))
    u_offset = jnp.clip(128.0 * jax.random.uniform(key_of[1], (CH, NBIN, BL), jnp.float32) ** block_scale(key_of[1], (CH, NBIN, BL), ((0, 2), (2, 16)), -0.2, 0.2), 0.0, 128.0)
    v_offset = jnp.clip(512.0 * jax.random.uniform(key_of[2], (CH, NBIN, BL), jnp.float32) ** block_scale(key_of[2], (CH, NBIN, BL), ((0, 2), (2, 16)), -0.2, 0.2), 0.0, 512.0)
    block_owner_keys = jax.random.split(jax.random.fold_in(key_of[3], 1), CH * BLOCKS // BLK_DEV)
    block_owner_turns = jax.random.permutation(jax.random.fold_in(key_of[3], 3), CH * BLOCKS // BLK_DEV)
    block_owner = jax.vmap(lambda own, number: shared_out(jax.random.fold_in(key_of[3], 2), own, number, BLK_DEV, N_UV, 1, MOST, 2))(block_owner_keys, block_owner_turns).reshape((CH, BLOCKS, 1))
    block_u_tile = with_ends(jax.random.randint(key_of[4], (CH, BLOCKS), 0, TILES), jax.random.fold_in(key_of[4], 1), 0, TILES - 1).astype(jnp.int32)
    block_count = with_ends(jax.random.randint(key_of[5], (CH, BLOCKS), VISIBILITY_ROWS // 8, VISIBILITY_ROWS + 1), jax.random.fold_in(key_of[5], 1), VISIBILITY_ROWS // 8, VISIBILITY_ROWS).astype(jnp.int32)
    sk_window = draw_sk_window(jax.random.fold_in(key_of[7], 71), 0)
    return {"visibilities": visibilities, "u_offset": u_offset, "v_offset": v_offset, "block_owner": block_owner, "block_u_tile": block_u_tile, "block_count": block_count, "sk_window": sk_window}


kernel_width = 1.3
ramp_width = 0.25

def kurtosis_weight(first_sum, second, window):
    ratio = SUBS * second / (first_sum * first_sum)
    kurtosis = (SUBS + 1.0) / (SUBS - 1.0) * (ratio - 1.0)
    lower = window[0].astype(jnp.float32) / 1000.0
    upper = window[1].astype(jnp.float32) / 1000.0
    return jnp.clip((kurtosis - lower) / ramp_width, 0.0, 1.0) * jnp.clip((upper - kurtosis) / ramp_width, 0.0, 1.0)

def block_rows(values):
    shaped = values.reshape(NBIN, N_UV, BL_DEV).transpose(1, 0, 2)
    return shaped.reshape(BLOCKS, VISIBILITY_ROWS)

def grid_tiles(payload):
    rows_v = jnp.arange(BAND).astype(jnp.float32)
    cols_u = jnp.arange(TILE).astype(jnp.float32)
    gap_v = rows_v[None, None, :] - payload[:, 3, :, None]
    gap_u = cols_u[None, None, :] - payload[:, 2, :, None]
    left = jnp.exp(-0.5 * gap_v * gap_v / (kernel_width * kernel_width)).astype(jnp.bfloat16)
    across = jnp.exp(-0.5 * gap_u * gap_u / (kernel_width * kernel_width))
    right = jnp.concatenate([payload[:, 0, :, None] * across, payload[:, 1, :, None] * across], axis=2).astype(jnp.bfloat16)
    return jnp.einsum('grj,gri->gji', left.astype(jnp.float32), right.astype(jnp.float32))

def taper(indices):
    offset = indices.astype(jnp.float32) - NI // 2
    scaled = offset / NG
    return jnp.exp(-2.0 * math.pi * math.pi * kernel_width * kernel_width * scaled * scaled)

def reference(visibilities, u_offset, v_offset, block_owner, block_u_tile, block_count, sk_window):
    group_size = math.gcd(BLOCKS, 256)
    select = jnp.concatenate([jnp.arange(NG - NI // 2, NG), jnp.arange(0, NI // 2)]).astype(jnp.int32)
    pixel_ids = jnp.arange(NI).astype(jnp.int32)
    sign_flip = 1.0 - 2.0 * ((pixel_ids[:, None] + pixel_ids[None, :]) % 2).astype(jnp.float32)
    row_taper = taper(pixel_ids)
    scale = 1.0 / math.sqrt(NBIN * BL)
    images = []
    for channel in range(CH):
        real_part = visibilities[:, :, channel, 0].astype(jnp.float32)
        imag_part = visibilities[:, :, channel, 1].astype(jnp.float32)
        powers = real_part * real_part + imag_part * imag_part
        sum_real = lax.optimization_barrier(jnp.sum(real_part, axis=1))
        imaginary_total = lax.optimization_barrier(jnp.sum(imag_part, axis=1))
        first_sum = lax.optimization_barrier(jnp.sum(powers, axis=1))
        second = lax.optimization_barrier(jnp.sum(powers * powers, axis=1))
        weight = kurtosis_weight(first_sum, second, sk_window[channel])
        avg_real = block_rows(weight * sum_real / SUBS)
        avg_imag = block_rows(weight * imaginary_total / SUBS)
        live_rows = jnp.arange(VISIBILITY_ROWS)[None, :] < block_count[channel][:, None]
        avg_real = jnp.where(live_rows, avg_real, 0.0)
        avg_imag = jnp.where(live_rows, avg_imag, 0.0)
        payload = jnp.stack([avg_real, avg_imag, block_rows(u_offset[channel]), block_rows(v_offset[channel])], axis=1)
        target = (block_owner[channel, :, 0] * TILES + block_u_tile[channel]).astype(jnp.int32)

        def accumulate(running, pieces):
            message_group, target_group = pieces
            return (running.at[target_group].add(grid_tiles(message_group)), None)
        uv_grid = jnp.zeros((N_UV * TILES, BAND, 2 * TILE), jnp.float32)
        uv_grid, _ = lax.scan(accumulate, uv_grid, (payload.reshape(-1, group_size, 4, VISIBILITY_ROWS), target.reshape(-1, group_size)))
        ordered = uv_grid.reshape(N_UV, TILES, BAND, 2, TILE).transpose(0, 2, 1, 3, 4)
        grid_real = ordered[:, :, :, 0, :].reshape(NG, NG)
        grid_imag = ordered[:, :, :, 1, :].reshape(NG, NG)
        spectrum = jnp.fft.ifft2(lax.complex(grid_real, grid_imag)) * (NG * NG)
        cropped = jnp.real(spectrum[select][:, select])
        images.append(cropped * sign_flip * scale / (row_taper[:, None] * row_taper[None, :]))
    return jnp.stack(images, axis=0)
```

```python
import functools
import math

import jax
import jax.numpy as jnp
import numpy as np
from jax import lax
from jax.experimental import pallas as pl
from jax.experimental.pallas import tpu as pltpu
from jax.sharding import PartitionSpec as P

NG = 8192
TILE = 128
VISIBILITY_ROWS = 128
SUBS = 16
NBIN = 8
BL_DEV = 2048
NI = 4096


kernel_width = 1.3
ramp_width = 0.25


def kurtosis_weight(first_sum, second, window):
    ratio = SUBS * second / (first_sum * first_sum)
    kurtosis = (SUBS + 1.0) / (SUBS - 1.0) * (ratio - 1.0)
    lower = window[0].astype(jnp.float32) / 1000.0
    upper = window[1].astype(jnp.float32) / 1000.0
    return jnp.clip((kurtosis - lower) / ramp_width, 0.0, 1.0) * jnp.clip(
        (upper - kurtosis) / ramp_width, 0.0, 1.0
    )


HALF = NG // 2
PAD = 16


def spread(gap):
    return jnp.exp(gap * gap * (-0.5 / (kernel_width * kernel_width)))


def grid_kernel(band, codes, first, spots, values, out, edge, picked):
    blocks = spots.shape[0]
    width = out.shape[2]
    base_w = first[0]
    step = 256

    def clear(at, carry):
        rows = pl.ds(pl.multiple_of(at * step, step), step)
        out[0, rows, :] = jnp.zeros((step, width), jnp.float32)
        out[1, rows, :] = jnp.zeros((step, width), jnp.float32)
        edge[rows, :] = jnp.zeros((step, TILE), jnp.float32)
        return carry

    lax.fori_loop(0, NG // step, clear, 0)

    def reach(tile):
        low = jnp.where(tile * TILE >= HALF, tile * TILE - HALF, HALF - tile * TILE - (TILE - 1))
        return low, (low < base_w + width) & (low + TILE > base_w)

    def pick(at, count):
        tile = lax.rem(codes[at], NG // TILE)
        _, mine = reach(tile)
        picked[count] = at
        return count + jnp.where(mine | (tile == 0), 1, 0)

    count = lax.fori_loop(0, blocks, pick, 0, unroll=8)
    tall = band + PAD
    p_ids = lax.broadcasted_iota(jnp.int32, (tall, VISIBILITY_ROWS), 0)
    w_ids = lax.broadcasted_iota(jnp.int32, (width, VISIBILITY_ROWS), 0)
    e_ids = lax.broadcasted_iota(jnp.int32, (TILE, VISIBILITY_ROWS), 0)

    def product(left, right):
        return lax.dot_general(
            left, right, (((1,), (1,)), ((), ())), preferred_element_type=jnp.float32
        )

    def add(at, carry):
        block = picked[at]
        code = codes[block]
        owner = lax.div(code, NG // TILE)
        tile = lax.rem(code, NG // TILE)
        low, mine = reach(tile)
        mirrored = tile * TILE < HALF
        sign = jnp.where(mirrored, -1, 1)
        eight = pl.ds(pl.multiple_of(lax.div(block, 8) * 8, 8), 8)
        here = lax.broadcasted_iota(jnp.int32, (8, 2 * TILE), 0) == lax.rem(block, 8)
        spot = jnp.sum(jnp.where(here, spots[eight, :], 0.0), axis=0, keepdims=True)
        value_row = jnp.sum(jnp.where(here, values[eight, :], 0.0), axis=0, keepdims=True)
        u, v = spot[:, :TILE], spot[:, TILE:]
        real, imag = value_row[:, :TILE], value_row[:, TILE:] * sign.astype(jnp.float32)
        j_ids = sign * p_ids + jnp.where(mirrored, band, 0)
        left = jnp.where(
            (j_ids >= 0) & (j_ids < band), spread(j_ids.astype(jnp.float32) - v), 0.0
        ).astype(jnp.bfloat16)
        start = jnp.where(mirrored, NG - band * (owner + 1), band * owner)
        main_rows = pl.ds(pl.multiple_of(start, band), band)
        last_rows = pl.ds(pl.multiple_of(lax.rem(start + band, NG), band), PAD)

        @pl.when(mine)
        def _():
            i_ids = sign * (w_ids + base_w - low) + jnp.where(mirrored, TILE - 1, 0)
            across = jnp.where(
                (i_ids >= 0) & (i_ids < TILE), spread(i_ids.astype(jnp.float32) - u), 0.0
            )
            for part, value in ((0, real), (1, imag)):
                made = product(left, (value * across).astype(jnp.bfloat16))
                out[part, main_rows, :] += made[:band]
                out[part, last_rows, :] += made[band:]

        @pl.when(tile == 0)
        def _():
            across = spread(u)
            right = jnp.where(
                e_ids == 0, real * across, jnp.where(e_ids == 1, imag * across, 0.0)
            ).astype(jnp.bfloat16)
            made = product(left, right)
            edge[main_rows, :] += made[:band]
            edge[last_rows, :] += made[band:]

        return carry

    lax.fori_loop(0, count, add, 0)


def grid_blocks(codes, first, spots, values, band, width):
    vmem = pl.BlockSpec(memory_space=pltpu.VMEM)
    smem = pl.BlockSpec(memory_space=pltpu.SMEM)
    return pl.pallas_call(
        functools.partial(grid_kernel, band),
        out_shape=(
            jax.ShapeDtypeStruct((2, NG, width), jnp.float32),
            jax.ShapeDtypeStruct((NG, TILE), jnp.float32),
        ),
        in_specs=[smem, smem, vmem, vmem],
        out_specs=(vmem, vmem),
        scratch_shapes=[pltpu.SMEM((spots.shape[0] + 8,), jnp.int32)],
        compiler_params=pltpu.CompilerParams(vmem_limit_bytes=56 * 1024 * 1024),
    )(codes, first, spots, values)


def taper(indices):
    offset = indices.astype(jnp.float32) - NI // 2
    scaled = offset / NG
    return jnp.exp(-2.0 * math.pi * math.pi * kernel_width * kernel_width * scaled * scaled)


def rotation(product, modulus):
    angles = (product % modulus) * (2.0 * math.pi / modulus)
    cos_part, sin_part = np.cos(angles), np.sin(angles)
    return np.stack(
        [np.stack([cos_part, sin_part], -1), np.stack([-sin_part, cos_part], -1)], -2
    ).astype(np.float32)


def transform_tables(inner, count):
    outer = NG // inner
    kept = NI // outer
    j_ids = np.arange(kept) - kept // 2
    k_ids = np.arange(outer)
    q_ids = np.arange(inner)
    one = rotation(np.arange(count)[:, None] * k_ids[None, :], outer)
    two = rotation(
        q_ids[None, :, None] * (k_ids[:, None, None] + outer * j_ids[None, None, :]), NG
    )
    return one, two


mix = functools.partial(
    jnp.einsum, precision=lax.Precision.HIGH, preferred_element_type=jnp.float32
)


def body(visibilities, u_offset, v_offset, block_owner, block_u_tile, block_count, sk_window):
    owners = lax.axis_size("uv")
    local_bin_count = visibilities.shape[0]
    antenna_pairs = visibilities.shape[4]
    local_block_count = local_bin_count * antenna_pairs // VISIBILITY_ROWS
    blocked = (local_block_count, VISIBILITY_ROWS)
    spots = lax.all_gather(
        jnp.concatenate([u_offset[0].reshape(blocked), v_offset[0].reshape(blocked)], axis=1),
        "uv",
        tiled=True,
    )
    codes = lax.all_gather(
        block_owner[0, :, 0] * (NG // TILE) + block_u_tile[0], "uv", tiled=True
    )
    real_part = visibilities[:, :, :, 0].astype(jnp.float32)
    imag_part = visibilities[:, :, :, 1].astype(jnp.float32)
    powers = real_part * real_part + imag_part * imag_part
    local_sums = jnp.stack(
        [
            jnp.sum(real_part, axis=1),
            jnp.sum(imag_part, axis=1),
            jnp.sum(powers, axis=1),
            jnp.sum(powers * powers, axis=1),
        ],
        axis=0,
    )
    local_sums = local_sums.transpose(2, 0, 1, 3)
    totals = lax.psum_scatter(local_sums, "tm", scatter_dimension=0, tiled=True)[0]
    weight = kurtosis_weight(totals[2], totals[3], sk_window[0])
    avg_real = (weight * totals[0] / SUBS).reshape(blocked)
    avg_imag = (weight * totals[1] / SUBS).reshape(blocked)
    live_rows = jnp.arange(VISIBILITY_ROWS)[None, :] < block_count[0][:, None]
    avg_real = jnp.where(live_rows, avg_real, 0.0)
    avg_imag = jnp.where(live_rows, avg_imag, 0.0)
    values = lax.all_gather(
        jnp.concatenate([avg_real, avg_imag], axis=1), "uv", tiled=True
    )
    band = NG // owners
    width = HALF // owners
    me = lax.axis_index("uv")
    uv_grid, edge = grid_blocks(
        codes, (me * width)[None].astype(jnp.int32), spots, values, band, width
    )

    outer = NG // TILE
    one, two = transform_tables(TILE, outer)
    rows_mine = NI // owners
    jj_mine = rows_mine // outer
    stage = mix("cnqw,nkcd->dkqw", uv_grid.reshape(2, outer, TILE, width), one)
    two_split = two.reshape(outer, TILE, owners, jj_mine, 2, 2)

    edge_in = edge[:, :2].T.reshape(2, outer, TILE)
    edge_stage = mix("cnq,nkcd->dkq", edge_in, one)
    edge_all = mix("ckq,kqjc->jk", edge_stage, two[..., 0])
    edge_mine = lax.dynamic_slice_in_dim(edge_all, me * jj_mine, jj_mine, 0).reshape(rows_mine)

    inner = min(width, TILE)
    per_owner = width // inner
    outer_l = NG // inner
    row_one, row_two = transform_tables(inner, HALF // inner)
    row_one = row_one.reshape(owners, per_owner, outer_l, 2, 2)
    row_two = row_two[..., 0]
    scale = 1.0 / math.sqrt(NBIN * BL_DEV * owners)
    col_ids = jnp.arange(NI)
    parts = 2 if jj_mine % 2 == 0 else 1
    jj_part = jj_mine // parts
    rows_part = rows_mine // parts
    images = []
    for part in range(parts):
        table = two_split[:, :, :, part * jj_part : (part + 1) * jj_part]
        columns = mix("ckqw,kqejcd->edjkw", stage, table)
        columns = columns.reshape(owners, 2, rows_part, per_owner, inner).transpose(0, 1, 3, 2, 4)
        columns = lax.all_to_all(columns, "uv", split_axis=0, concat_axis=0, tiled=True)
        row_stage = mix("scnmq,snkcd->dkmq", columns, row_one)
        image = mix("ckmq,kqjc->mjk", row_stage, row_two).reshape(rows_part, NI)
        row_ids = me * rows_mine + part * rows_part + jnp.arange(rows_part)
        edge_part = edge_mine[part * rows_part : (part + 1) * rows_part]
        col_sign = 1.0 - 2.0 * (col_ids % 2).astype(jnp.float32)
        row_sign = 1.0 - 2.0 * (row_ids % 2).astype(jnp.float32)
        image = image + edge_part[:, None] * col_sign[None, :]
        row_factor = row_sign * scale / taper(row_ids)
        images.append(image * row_factor[:, None] / taper(col_ids)[None, :])
    return jnp.concatenate(images, axis=0)[None]


def solution(mesh):
    placed = (
        P(None, "tm", None, None, "uv"),
        P("tm", None, "uv"),
        P("tm", None, "uv"),
        P("tm", "uv", None),
        P("tm", "uv"),
        P("tm", "uv"),
        P("tm", None),
    )
    return jax.shard_map(
        body, mesh=mesh, in_specs=placed, out_specs=P("tm", "uv", None), check_vma=False
    )
```

```python
import functools
import math

import jax
import jax.numpy as jnp
import numpy as np
from jax import lax
from jax.experimental import pallas as pl
from jax.experimental.pallas import tpu as pltpu
from jax.sharding import PartitionSpec as P

NG = 8192
TILE = 128
VISIBILITY_ROWS = 128
SUBS = 16
NBIN = 8
BL_DEV = 2048
NI = 4096


kernel_width = 1.3
ramp_width = 0.25


def kurtosis_weight(first_sum, second, window):
    ratio = SUBS * second / (first_sum * first_sum)
    kurtosis = (SUBS + 1.0) / (SUBS - 1.0) * (ratio - 1.0)
    lower = window[0].astype(jnp.float32) / 1000.0
    upper = window[1].astype(jnp.float32) / 1000.0
    return jnp.clip((kurtosis - lower) / ramp_width, 0.0, 1.0) * jnp.clip(
        (upper - kurtosis) / ramp_width, 0.0, 1.0
    )


HALF = NG // 2
PAD = 16


def spread(gap):
    return jnp.exp(gap * gap * (-0.5 / (kernel_width * kernel_width)))


def reach(tile, first, width):
    low = jnp.where(tile * TILE >= HALF, tile * TILE - HALF, HALF - tile * TILE - (TILE - 1))
    return low, (low < first + width) & (low + TILE > first)


def grid_kernel(band, group, skip, codes, first, payload, out, edge, picked):
    blocks = codes.shape[0]
    width = out.shape[2]
    base_w = first[0]
    step = 256

    def clear(at, carry):
        rows = pl.ds(pl.multiple_of(at * step, step), step)
        out[0, rows, :] = jnp.zeros((step, width), jnp.float32)
        out[1, rows, :] = jnp.zeros((step, width), jnp.float32)
        edge[rows, :] = jnp.zeros((step, TILE), jnp.float32)
        return carry

    lax.fori_loop(0, NG // step, clear, 0)

    def pick(at, count):
        tile = lax.rem(codes[at], NG // TILE)
        _, mine = reach(tile, base_w, width)
        picked[count] = at
        return count + jnp.where(mine | (tile == 0), 1, 0)

    count = lax.fori_loop(0, blocks, pick, 0, unroll=8)
    tall = band + PAD
    piece = min(width, TILE)
    p_ids = lax.broadcasted_iota(jnp.int32, (tall, VISIBILITY_ROWS), 0)
    w_ids = lax.broadcasted_iota(jnp.int32, (piece, VISIBILITY_ROWS), 0)
    e_ids = lax.broadcasted_iota(jnp.int32, (TILE, VISIBILITY_ROWS), 0)

    def product(left, right):
        return lax.dot_general(
            left, right, (((1,), (1,)), ((), ())), preferred_element_type=jnp.float32
        )

    def add(at, carry):
        block = picked[at]
        code = codes[block]
        owner = lax.div(code, NG // TILE)
        tile = lax.rem(code, NG // TILE)
        low, _ = reach(tile, base_w, width)
        mirrored = tile * TILE < HALF
        sign = jnp.where(mirrored, -1, 1)
        row = block + skip * lax.div(block, group)
        eight = pl.ds(pl.multiple_of(lax.div(row, 8) * 8, 8), 8)
        here = lax.broadcasted_iota(jnp.int32, (8, 4 * TILE), 0) == lax.rem(row, 8)
        fields = jnp.sum(jnp.where(here, payload[eight, :], 0.0), axis=0, keepdims=True)
        real = fields[:, :TILE]
        imag = fields[:, TILE : 2 * TILE] * sign.astype(jnp.float32)
        u = fields[:, 2 * TILE : 3 * TILE]
        v = fields[:, 3 * TILE :]
        centre = jnp.where(mirrored, band - v, v)
        least = jnp.where(mirrored, 1, 0)
        left = jnp.where(
            (p_ids >= least) & (p_ids < band + least),
            spread(p_ids.astype(jnp.float32) - centre),
            0.0,
        ).astype(jnp.bfloat16)
        start = jnp.where(mirrored, NG - band * (owner + 1), band * owner)
        main_rows = pl.ds(pl.multiple_of(start, band), band)
        last_rows = pl.ds(pl.multiple_of(lax.rem(start + band, NG), band), PAD)

        for at_w in range(0, width, piece):
            columns = slice(at_w, at_w + piece)

            @pl.when(reach(tile, base_w + at_w, piece)[1])
            def _():
                i_ids = sign * (w_ids + (base_w + at_w) - low) + jnp.where(mirrored, TILE - 1, 0)
                across = jnp.where(
                    (i_ids >= 0) & (i_ids < TILE), spread(i_ids.astype(jnp.float32) - u), 0.0
                )
                right = jnp.concatenate([real * across, imag * across], axis=0)
                made = product(left, right.astype(jnp.bfloat16))
                for part in (0, 1):
                    mine = made[:, part * piece : (part + 1) * piece]
                    out[part, main_rows, columns] += mine[:band]
                    out[part, last_rows, columns] += mine[band:]

        @pl.when(tile == 0)
        def _():
            across = spread(u)
            right = jnp.where(
                e_ids == 0, real * across, jnp.where(e_ids == 1, imag * across, 0.0)
            ).astype(jnp.bfloat16)
            made = product(left, right)
            edge[main_rows, :] += made[:band]
            edge[last_rows, :] += made[band:]

        return carry

    lax.fori_loop(0, count, add, 0)


def grid_blocks(codes, first, payload, band, width, group, skip):
    vmem = pl.BlockSpec(memory_space=pltpu.VMEM)
    smem = pl.BlockSpec(memory_space=pltpu.SMEM)
    return pl.pallas_call(
        functools.partial(grid_kernel, band, group, skip),
        out_shape=(
            jax.ShapeDtypeStruct((2, NG, width), jnp.float32),
            jax.ShapeDtypeStruct((NG, TILE), jnp.float32),
        ),
        in_specs=[smem, smem, vmem],
        out_specs=(vmem, vmem),
        scratch_shapes=[pltpu.SMEM((codes.shape[0] + 8,), jnp.int32)],
        compiler_params=pltpu.CompilerParams(vmem_limit_bytes=56 * 1024 * 1024),
    )(codes, first, payload)


def taper(indices):
    offset = indices.astype(jnp.float32) - NI // 2
    scaled = offset / NG
    return jnp.exp(-2.0 * math.pi * math.pi * kernel_width * kernel_width * scaled * scaled)


def rotation(product, modulus):
    angles = (product % modulus) * (2.0 * math.pi / modulus)
    cos_part, sin_part = np.cos(angles), np.sin(angles)
    return np.stack(
        [np.stack([cos_part, sin_part], -1), np.stack([-sin_part, cos_part], -1)], -2
    ).astype(np.float32)


def transform_tables(inner, count):
    outer = NG // inner
    kept = NI // outer
    j_ids = np.arange(kept) - kept // 2
    k_ids = np.arange(outer)
    q_ids = np.arange(inner)
    one = rotation(np.arange(count)[:, None] * k_ids[None, :], outer)
    two = rotation(
        q_ids[None, :, None] * (k_ids[:, None, None] + outer * j_ids[None, None, :]), NG
    )
    return one, two


mix = functools.partial(
    jnp.einsum, precision=lax.Precision.HIGH, preferred_element_type=jnp.float32
)


def body(visibilities, u_offset, v_offset, block_owner, block_u_tile, block_count, sk_window):
    owners = lax.axis_size("uv")
    local_bin_count = visibilities.shape[0]
    antenna_pairs = visibilities.shape[4]
    local_block_count = local_bin_count * antenna_pairs // VISIBILITY_ROWS
    blocked = (local_block_count, VISIBILITY_ROWS)
    band = NG // owners
    width = HALF // owners
    me = lax.axis_index("uv")
    tiles = block_u_tile[0]
    codes = block_owner[0, :, 0] * (NG // TILE) + tiles
    room = min(local_block_count, -(-(16 + 2 * local_block_count // owners) // 8) * 8)
    starts = jnp.arange(owners)[:, None] * width
    wanted = reach(tiles[None, :], starts, width)[1] | (tiles[None, :] == 0)
    ranks = jnp.cumsum(wanted.astype(jnp.int32), axis=1) - 1
    fullest = lax.pmax(jnp.max(ranks) + 1, ("tm", "uv"))
    chosen = wanted[:, None, :] & (ranks[:, None, :] == jnp.arange(room)[None, :, None])
    sent_codes = jnp.sum(jnp.where(chosen, codes + 1, 0), axis=2)
    real_part = visibilities[:, :, :, 0].astype(jnp.float32)
    imag_part = visibilities[:, :, :, 1].astype(jnp.float32)
    powers = real_part * real_part + imag_part * imag_part
    local_sums = jnp.stack(
        [
            jnp.sum(real_part, axis=1),
            jnp.sum(imag_part, axis=1),
            jnp.sum(powers, axis=1),
            jnp.sum(powers * powers, axis=1),
        ],
        axis=0,
    )
    local_sums = local_sums.transpose(2, 0, 1, 3)
    totals = lax.psum_scatter(local_sums, "tm", scatter_dimension=0, tiled=True)[0]
    weight = kurtosis_weight(totals[2], totals[3], sk_window[0])
    avg_real = (weight * totals[0] / SUBS).reshape(blocked)
    avg_imag = (weight * totals[1] / SUBS).reshape(blocked)
    live_rows = jnp.arange(VISIBILITY_ROWS)[None, :] < block_count[0][:, None]
    avg_real = jnp.where(live_rows, avg_real, 0.0)
    avg_imag = jnp.where(live_rows, avg_imag, 0.0)
    payload = jnp.concatenate(
        [avg_real, avg_imag, u_offset[0].reshape(blocked), v_offset[0].reshape(blocked)], axis=1
    )
    first = (me * width)[None].astype(jnp.int32)

    def to_reached(payload):
        sent = jnp.einsum(
            "esb,bf->esf", chosen.astype(jnp.float32), payload, precision=lax.Precision.HIGHEST
        )
        line = jnp.pad(sent_codes.astype(jnp.float32), ((0, 0), (0, payload.shape[1] - room)))
        lines = jnp.pad(line[:, None, :], ((0, 0), (0, 7), (0, 0)))
        got = lax.all_to_all(
            jnp.concatenate([sent, lines], axis=1), "uv", split_axis=0, concat_axis=0, tiled=True
        )
        got_codes = got[:, room, :room].astype(jnp.int32).reshape(-1) - 1
        rows = got.reshape(owners * (room + 8), payload.shape[1])
        return grid_blocks(got_codes, first, rows, band, width, room, 8)

    def to_all(payload):
        every = lax.all_gather(payload, "uv", tiled=True)
        every_code = lax.all_gather(codes, "uv", tiled=True)
        return grid_blocks(every_code, first, every, band, width, local_block_count, 0)

    uv_grid, edge = lax.cond(fullest <= room, to_reached, to_all, payload)

    outer = NG // TILE
    one, two = transform_tables(TILE, outer)
    rows_mine = NI // owners
    jj_mine = rows_mine // outer
    stage = mix("cnqw,nkcd->dkqw", uv_grid.reshape(2, outer, TILE, width), one)
    two_split = two.reshape(outer, TILE, owners, jj_mine, 2, 2)

    edge_in = edge[:, :2].T.reshape(2, outer, TILE)
    edge_stage = mix("cnq,nkcd->dkq", edge_in, one)
    edge_all = mix("ckq,kqjc->jk", edge_stage, two[..., 0])
    edge_mine = lax.dynamic_slice_in_dim(edge_all, me * jj_mine, jj_mine, 0).reshape(rows_mine)

    inner = min(width, TILE)
    per_owner = width // inner
    outer_l = NG // inner
    row_one, row_two = transform_tables(inner, HALF // inner)
    row_one = row_one.reshape(owners, per_owner, outer_l, 2, 2)
    row_two = row_two[..., 0]
    scale = 1.0 / math.sqrt(NBIN * BL_DEV * owners)
    col_ids = jnp.arange(NI)
    quarter = jj_mine // 4
    parts = (quarter, 2 * quarter, quarter) if jj_mine % 4 == 0 else (jj_mine,)
    images = []
    jj_done = 0
    for jj_part in parts:
        rows_part = jj_part * outer
        rows_done = jj_done * outer
        table = two_split[:, :, :, jj_done : jj_done + jj_part]
        jj_done += jj_part
        columns = mix("ckqw,kqejcd->edjkw", stage, table)
        columns = columns.reshape(owners, 2, rows_part, per_owner, inner).transpose(0, 1, 3, 2, 4)
        columns = lax.all_to_all(columns, "uv", split_axis=0, concat_axis=0, tiled=True)
        row_stage = mix("scnmq,snkcd->dkmq", columns, row_one)
        image = mix("ckmq,kqjc->mjk", row_stage, row_two).reshape(rows_part, NI)
        row_ids = me * rows_mine + rows_done + jnp.arange(rows_part)
        edge_part = edge_mine[rows_done : rows_done + rows_part]
        col_sign = 1.0 - 2.0 * (col_ids % 2).astype(jnp.float32)
        row_sign = 1.0 - 2.0 * (row_ids % 2).astype(jnp.float32)
        image = image + edge_part[:, None] * col_sign[None, :]
        row_factor = row_sign * scale / taper(row_ids)
        images.append(image * row_factor[:, None] / taper(col_ids)[None, :])
    return jnp.concatenate(images, axis=0)[None]


def solution(mesh):
    placed = (
        P(None, "tm", None, None, "uv"),
        P("tm", None, "uv"),
        P("tm", None, "uv"),
        P("tm", "uv", None),
        P("tm", "uv"),
        P("tm", "uv"),
        P("tm", None),
    )
    return jax.shard_map(
        body, mesh=mesh, in_specs=placed, out_specs=P("tm", "uv", None), check_vma=False
    )
```

```python
import functools
import math

import jax
import jax.numpy as jnp
import numpy as np
from jax import lax
from jax.experimental import pallas as pl
from jax.experimental.pallas import tpu as pltpu
from jax.sharding import PartitionSpec as P

NG = 8192
TILE = 128
VISIBILITY_ROWS = 128
SUBS = 16
NBIN = 8
BL_DEV = 2048
NI = 4096


kernel_width = 1.3
ramp_width = 0.25


def kurtosis_weight(first_sum, second, window):
    ratio = SUBS * second / (first_sum * first_sum)
    kurtosis = (SUBS + 1.0) / (SUBS - 1.0) * (ratio - 1.0)
    lower = window[0].astype(jnp.float32) / 1000.0
    upper = window[1].astype(jnp.float32) / 1000.0
    return jnp.clip((kurtosis - lower) / ramp_width, 0.0, 1.0) * jnp.clip(
        (upper - kurtosis) / ramp_width, 0.0, 1.0
    )


HALF = NG // 2
PAD = 16


def spread(gap):
    return jnp.exp(gap * gap * (-0.5 / (kernel_width * kernel_width)))


def reach(tile, first, width):
    low = jnp.where(tile * TILE >= HALF, tile * TILE - HALF, HALF - tile * TILE - (TILE - 1))
    return low, (low < first + width) & (low + TILE > first)


def grid_kernel(band, group, skip, codes, first, payload, out, edge, picked):
    blocks = codes.shape[0]
    width = out.shape[2]
    base_w = first[0]
    step = 256

    def clear(at, carry):
        rows = pl.ds(pl.multiple_of(at * step, step), step)
        out[0, rows, :] = jnp.zeros((step, width), jnp.float32)
        out[1, rows, :] = jnp.zeros((step, width), jnp.float32)
        edge[rows, :] = jnp.zeros((step, TILE), jnp.float32)
        return carry

    lax.fori_loop(0, NG // step, clear, 0)

    def pick(at, count):
        tile = lax.rem(codes[at], NG // TILE)
        _, mine = reach(tile, base_w, width)
        picked[count] = at
        return count + jnp.where(mine | (tile == 0), 1, 0)

    count = lax.fori_loop(0, blocks, pick, 0, unroll=8)
    tall = band + PAD
    piece = min(width, TILE)
    p_ids = lax.broadcasted_iota(jnp.int32, (tall, VISIBILITY_ROWS), 0)
    w_ids = lax.broadcasted_iota(jnp.int32, (piece, VISIBILITY_ROWS), 0)
    e_ids = lax.broadcasted_iota(jnp.int32, (TILE, VISIBILITY_ROWS), 0)

    def product(left, right):
        return lax.dot_general(
            left, right, (((1,), (1,)), ((), ())), preferred_element_type=jnp.float32
        )

    def add(at, carry):
        block = picked[at]
        code = codes[block]
        owner = lax.div(code, NG // TILE)
        tile = lax.rem(code, NG // TILE)
        low, _ = reach(tile, base_w, width)
        mirrored = tile * TILE < HALF
        sign = jnp.where(mirrored, -1, 1)
        row = block + skip * lax.div(block, group)
        eight = pl.ds(pl.multiple_of(lax.div(row, 8) * 8, 8), 8)
        here = lax.broadcasted_iota(jnp.int32, (8, 4 * TILE), 0) == lax.rem(row, 8)
        fields = jnp.sum(jnp.where(here, payload[eight, :], 0.0), axis=0, keepdims=True)
        real = fields[:, :TILE]
        imag = fields[:, TILE : 2 * TILE] * sign.astype(jnp.float32)
        u = fields[:, 2 * TILE : 3 * TILE]
        v = fields[:, 3 * TILE :]
        centre = jnp.where(mirrored, band - v, v)
        least = jnp.where(mirrored, 1, 0)
        left = jnp.where(
            (p_ids >= least) & (p_ids < band + least),
            spread(p_ids.astype(jnp.float32) - centre),
            0.0,
        ).astype(jnp.bfloat16)
        start = jnp.where(mirrored, NG - band * (owner + 1), band * owner)
        main_rows = pl.ds(pl.multiple_of(start, band), band)
        last_rows = pl.ds(pl.multiple_of(lax.rem(start + band, NG), band), PAD)

        for at_w in range(0, width, piece):
            columns = slice(at_w, at_w + piece)

            @pl.when(reach(tile, base_w + at_w, piece)[1])
            def _():
                i_ids = sign * (w_ids + (base_w + at_w) - low) + jnp.where(mirrored, TILE - 1, 0)
                across = jnp.where(
                    (i_ids >= 0) & (i_ids < TILE), spread(i_ids.astype(jnp.float32) - u), 0.0
                )
                right = jnp.concatenate([real * across, imag * across], axis=0)
                made = product(left, right.astype(jnp.bfloat16))
                for part in (0, 1):
                    mine = made[:, part * piece : (part + 1) * piece]
                    out[part, main_rows, columns] += mine[:band]
                    out[part, last_rows, columns] += mine[band:]

        @pl.when(tile == 0)
        def _():
            across = spread(u)
            right = jnp.where(
                e_ids == 0, real * across, jnp.where(e_ids == 1, imag * across, 0.0)
            ).astype(jnp.bfloat16)
            made = product(left, right)
            edge[main_rows, :] += made[:band]
            edge[last_rows, :] += made[band:]

        return carry

    lax.fori_loop(0, count, add, 0)


def grid_blocks(codes, first, payload, band, width, group, skip):
    vmem = pl.BlockSpec(memory_space=pltpu.VMEM)
    smem = pl.BlockSpec(memory_space=pltpu.SMEM)
    return pl.pallas_call(
        functools.partial(grid_kernel, band, group, skip),
        out_shape=(
            jax.ShapeDtypeStruct((2, NG, width), jnp.float32),
            jax.ShapeDtypeStruct((NG, TILE), jnp.float32),
        ),
        in_specs=[smem, smem, vmem],
        out_specs=(vmem, vmem),
        scratch_shapes=[pltpu.SMEM((codes.shape[0] + 8,), jnp.int32)],
        compiler_params=pltpu.CompilerParams(vmem_limit_bytes=56 * 1024 * 1024),
    )(codes, first, payload)


def taper(indices):
    offset = indices.astype(jnp.float32) - NI // 2
    scaled = offset / NG
    return jnp.exp(-2.0 * math.pi * math.pi * kernel_width * kernel_width * scaled * scaled)


def rotation(product, modulus):
    angles = (product % modulus) * (2.0 * math.pi / modulus)
    cos_part, sin_part = np.cos(angles), np.sin(angles)
    return np.stack(
        [np.stack([cos_part, sin_part], -1), np.stack([-sin_part, cos_part], -1)], -2
    ).astype(np.float32)


def transform_tables(inner, count):
    outer = NG // inner
    kept = NI // outer
    j_ids = np.arange(kept) - kept // 2
    k_ids = np.arange(outer)
    q_ids = np.arange(inner)
    one = rotation(np.arange(count)[:, None] * k_ids[None, :], outer)
    two = rotation(
        q_ids[None, :, None] * (k_ids[:, None, None] + outer * j_ids[None, None, :]), NG
    )
    return one, two


mix = functools.partial(
    jnp.einsum, precision=lax.Precision.HIGH, preferred_element_type=jnp.float32
)


def body(visibilities, u_offset, v_offset, block_owner, block_u_tile, block_count, sk_window):
    owners = lax.axis_size("uv")
    local_bin_count = visibilities.shape[0]
    antenna_pairs = visibilities.shape[4]
    local_block_count = local_bin_count * antenna_pairs // VISIBILITY_ROWS
    blocked = (local_block_count, VISIBILITY_ROWS)
    band = NG // owners
    width = HALF // owners
    me = lax.axis_index("uv")
    tiles = block_u_tile[0]
    codes = block_owner[0, :, 0] * (NG // TILE) + tiles
    room = min(local_block_count, -(-(16 + 2 * local_block_count // owners) // 8) * 8)
    starts = jnp.arange(owners)[:, None] * width
    wanted = reach(tiles[None, :], starts, width)[1] | (tiles[None, :] == 0)
    ranks = jnp.cumsum(wanted.astype(jnp.int32), axis=1) - 1
    too_many = (jnp.max(ranks) + 1 > room).astype(jnp.float32)
    chosen = wanted[:, None, :] & (ranks[:, None, :] == jnp.arange(room)[None, :, None])
    sent_codes = jnp.sum(jnp.where(chosen, codes + 1, 0), axis=2)
    real_part = visibilities[:, :, :, 0].astype(jnp.float32)
    imag_part = visibilities[:, :, :, 1].astype(jnp.float32)
    powers = real_part * real_part + imag_part * imag_part
    local_sums = jnp.stack(
        [
            jnp.sum(real_part, axis=1),
            jnp.sum(imag_part, axis=1),
            jnp.sum(powers, axis=1),
            jnp.sum(powers * powers, axis=1),
        ],
        axis=0,
    )
    local_sums = local_sums.transpose(2, 0, 1, 3)
    flag_plane = jnp.broadcast_to(too_many, local_sums[:, :1].shape)
    local_sums = jnp.concatenate([local_sums, flag_plane], axis=1)
    totals = lax.psum_scatter(local_sums, "tm", scatter_dimension=0, tiled=True)[0]
    weight = kurtosis_weight(totals[2], totals[3], sk_window[0])
    avg_real = (weight * totals[0] / SUBS).reshape(blocked)
    avg_imag = (weight * totals[1] / SUBS).reshape(blocked)
    live_rows = jnp.arange(VISIBILITY_ROWS)[None, :] < block_count[0][:, None]
    avg_real = jnp.where(live_rows, avg_real, 0.0)
    avg_imag = jnp.where(live_rows, avg_imag, 0.0)
    payload = jnp.concatenate(
        [avg_real, avg_imag, u_offset[0].reshape(blocked), v_offset[0].reshape(blocked)], axis=1
    )
    first = (me * width)[None].astype(jnp.int32)

    sent = jnp.einsum(
        "esb,bf->esf", chosen.astype(jnp.float32), payload, precision=lax.Precision.HIGHEST
    )
    line = jnp.concatenate(
        [
            sent_codes.astype(jnp.float32),
            jnp.broadcast_to(totals[4, 0, 0], (owners, payload.shape[1] - room)),
        ],
        axis=1,
    )
    lines = jnp.pad(line[:, None, :], ((0, 0), (0, 7), (0, 0)))
    got = lax.all_to_all(
        jnp.concatenate([sent, lines], axis=1), "uv", split_axis=0, concat_axis=0, tiled=True
    )
    overfull = jnp.max(got[:, room, room])

    def from_reaching(got, payload):
        got_codes = got[:, room, :room].astype(jnp.int32).reshape(-1) - 1
        rows = got.reshape(owners * (room + 8), payload.shape[1])
        return grid_blocks(got_codes, first, rows, band, width, room, 8)

    def from_all(got, payload):
        every = lax.all_gather(payload, "uv", tiled=True)
        every_code = lax.all_gather(codes, "uv", tiled=True)
        return grid_blocks(every_code, first, every, band, width, local_block_count, 0)

    uv_grid, edge = lax.cond(overfull < 0.5, from_reaching, from_all, got, payload)

    outer = NG // TILE
    one, two = transform_tables(TILE, outer)
    rows_mine = NI // owners
    jj_mine = rows_mine // outer
    stage = mix("cnqw,nkcd->dkqw", uv_grid.reshape(2, outer, TILE, width), one)
    two_split = two.reshape(outer, TILE, owners, jj_mine, 2, 2)

    edge_in = edge[:, :2].T.reshape(2, outer, TILE)
    edge_stage = mix("cnq,nkcd->dkq", edge_in, one)
    edge_all = mix("ckq,kqjc->jk", edge_stage, two[..., 0])
    edge_mine = lax.dynamic_slice_in_dim(edge_all, me * jj_mine, jj_mine, 0).reshape(rows_mine)

    inner = min(width, TILE)
    per_owner = width // inner
    outer_l = NG // inner
    row_one, row_two = transform_tables(inner, HALF // inner)
    row_one = row_one.reshape(owners, per_owner, outer_l, 2, 2)
    row_two = row_two[..., 0]
    scale = 1.0 / math.sqrt(NBIN * BL_DEV * owners)
    col_ids = jnp.arange(NI)
    quarter = jj_mine // 4
    parts = (quarter, 2 * quarter, quarter) if jj_mine % 4 == 0 else (jj_mine,)
    images = []
    jj_done = 0
    for jj_part in parts:
        rows_part = jj_part * outer
        rows_done = jj_done * outer
        table = two_split[:, :, :, jj_done : jj_done + jj_part]
        jj_done += jj_part
        columns = mix("ckqw,kqejcd->edjkw", stage, table)
        columns = columns.reshape(owners, 2, rows_part, per_owner, inner).transpose(0, 1, 3, 2, 4)
        columns = lax.all_to_all(columns, "uv", split_axis=0, concat_axis=0, tiled=True)
        row_stage = mix("scnmq,snkcd->dkmq", columns, row_one)
        image = mix("ckmq,kqjc->mjk", row_stage, row_two).reshape(rows_part, NI)
        row_ids = me * rows_mine + rows_done + jnp.arange(rows_part)
        edge_part = edge_mine[rows_done : rows_done + rows_part]
        col_sign = 1.0 - 2.0 * (col_ids % 2).astype(jnp.float32)
        row_sign = 1.0 - 2.0 * (row_ids % 2).astype(jnp.float32)
        image = image + edge_part[:, None] * col_sign[None, :]
        row_factor = row_sign * scale / taper(row_ids)
        images.append(image * row_factor[:, None] / taper(col_ids)[None, :])
    return jnp.concatenate(images, axis=0)[None]


def solution(mesh):
    placed = (
        P(None, "tm", None, None, "uv"),
        P("tm", None, "uv"),
        P("tm", None, "uv"),
        P("tm", "uv", None),
        P("tm", "uv"),
        P("tm", "uv"),
        P("tm", None),
    )
    return jax.shard_map(
        body, mesh=mesh, in_specs=placed, out_specs=P("tm", "uv", None), check_vma=False
    )
```
